32 devices in a mesh: section: 8 (over z, x), expert: 4 (over y, core).
Axes of the slice: x: 2, y: 2, z: 4, core: 2. Of those that a mesh axis runs over, the one named last changes fastest.
Arguments:
- tokens: bfloat16 [1024, 4096], P('expert', 'section'), may hold values from -6 to 6
- routes: int32 [1024, 2], P('expert'), may hold values from 0 to 3, all different within a row; in each aligned block of 256 rows (0 to 255, 256 to 511, ...) at most 160 rows name the same one
- mix_weights: float32 [1024, 2], P('expert'), may hold values from 0.2 to 1
- w_gate: bfloat16 [4, 4096, 8192], P('expert', None, 'section'), may hold values from -0.125 to 0.125
- w_up: bfloat16 [4, 4096, 8192], P('expert', None, 'section'), may hold values from -0.125 to 0.125
- w_down: bfloat16 [4, 8192, 4096], P('expert', 'section'), may hold values from -0.09375 to 0.09375
- upstream: bfloat16 [1024, 4096], P('expert', 'section'), may hold values from -6 to 6
Outputs:
- mixed: bfloat16 [1024, 4096], P('expert', 'section')
- grad_tokens: bfloat16 [1024, 4096], P('expert', 'section')
- grad_mix: float32 [1024, 2], P('expert')
- grad_gate: bfloat16 [4, 4096, 8192], P('expert', None, 'section')
- grad_up: bfloat16 [4, 4096, 8192], P('expert', None, 'section')
- grad_down: bfloat16 [4, 8192, 4096], P('expert', 'section')
The draws below stay inside these ranges and needn't reach their ends.
Inputs may be any that keep to these rules, and one draw needn't show every extreme that they name: `routes`: each token names 2 different experts. Among the 256 tokens of one index of the expert axis no expert is named more than 160 times, and in some such block one expert is named exactly 160 times.
All inputs are finite; a program needn't handle non-finite values.
Results may differ from the reference program's by a relative error of at most 0.02.
Values may be sent and summed in bfloat16 or wider, within the bound.
A program may use at most 128 MiB of HBM per device.

```python
import math
import jax
import jax.numpy as jnp
import numpy as np
from jax import lax

D = 4096
FF = 8192
NEXP = 4
TOP = 2
TOK_DEV = 256
CAP = 160
TOKENS = 1024
N_SECTION = 8
N_EXPERT = 4


def strengthened(entries, stream_key, source, target, blocks, factor):
    def block_of(dim):
        return (jnp.arange(entries.shape[dim]) // (entries.shape[dim] // blocks)).reshape((-1,) + (1,) * (entries.ndim - 1 - dim))

    near = jax.random.permutation(stream_key, blocks)[block_of(target)]
    far = (block_of(target) + blocks // 2) % blocks
    return jnp.where((block_of(source) == near) | (block_of(source) == far), factor * entries, entries)


def block_scale(key, dims, cuts, smallest, top_value):
    level, own = 1.0, jax.random.fold_in(key, 6)
    for dim, blocks in cuts:
        draws = jnp.exp(jax.random.uniform(jax.random.fold_in(own, dim), (blocks,), jnp.float32, smallest / len(cuts), top_value / len(cuts)))
        level = level * jnp.repeat(draws, dims[dim] // blocks).reshape([-1 if axis == dim else 1 for axis in range(len(dims))])
    return level


def routed_block(key, own, number, rows, number_of, top, bound, slope):
    sequence = jax.random.permutation(key, number_of)
    crowded, ordinary = portions_of(number_of, rows * top, bound, slope, True), portions_of(number_of, rows * top, bound, slope, False)
    places = jnp.arange(number_of)

    def named(tallies, rotation):
        used = int((tallies > 0).sum())
        fixed = max(1, used // 4)
        moved = fixed + (places - fixed + rotation * (used - fixed)) % max(1, number_of - fixed)
        return jnp.zeros((number_of,), jnp.int32).at[sequence[jnp.where(places < fixed, places, moved)]].set(jnp.asarray(tallies, jnp.int32))

    tallies = jnp.where(number % 4 == 0, named(crowded, number // 4), named(ordinary, number - number // 4 - 1))
    mixed = jax.random.permutation(jax.random.fold_in(own, 3), number_of)
    donor, receiver = mixed[0:number_of // 2 * 2:2], mixed[1:number_of // 2 * 2:2]
    slack = jnp.minimum(tallies[donor] - 1, bound - tallies[receiver]) // 2
    slack = jnp.where((donor == sequence[0]) | (receiver == sequence[0]) | (tallies[receiver] == 0), 0, jnp.maximum(slack, 0))
    moved = jax.random.randint(jax.random.fold_in(own, 4), (number_of // 2,), 0, 1 << 20) % (slack + 1)
    tallies = tallies.at[donor].add(-moved).at[receiver].add(moved)
    items = jnp.searchsorted(jnp.cumsum(tallies), jnp.arange(rows * top), side="right").astype(jnp.int32)
    listing = items.reshape(top, rows).T
    listing = listing[jax.random.permutation(jax.random.fold_in(own, 1), rows)]
    rotation = jax.random.randint(jax.random.fold_in(own, 2), (rows, 1), 0, top)
    return jnp.take_along_axis(listing, (jnp.arange(top)[None, :] + rotation) % top, axis=1)


def portions_of(amount, total, bound, lean, full):
    loads = [(1 << 20) // math.isqrt(grade ** lean) + 1 for grade in range(1, amount + 1)]
    largest = bound if full else min(bound, max(-(-total // amount), total * loads[0] // sum(loads)))
    least = 1 if total - largest >= amount - 1 else 0
    given, spare = [largest] + [least] * (amount - 1), total - largest - least * (amount - 1)
    while spare > 0:
        free = [i for i in range(1, amount) if given[i] < largest] or [i for i in range(1, amount) if given[i] < bound]
        whole, left = sum([loads[i] for i in free]), spare
        for i in free:
            extra = min(bound - given[i], max(1, left * loads[i] // whole), spare)
            given[i] = given[i] + extra
            spare = spare - extra
    return np.array(given)


def gaussian(own_key, dims, width, bound, cuts=(), held_as=jnp.bfloat16):
    result = jax.random.normal(own_key, dims, jnp.float32) * width
    if len(cuts) > 0:
        result = block_scale(own_key, dims, cuts, -0.22, 0.18) * result
    return jnp.clip(result, min=-bound, max=bound).astype(held_as)


def heavy_noise(own_key, extent, deviation, reach, pieces, heavy, kind=jnp.bfloat16):
    array = deviation * jax.random.normal(own_key, extent, jnp.float32)
    if pieces:
        array = array * block_scale(own_key, extent, pieces, -0.22, 0.18)
    return jnp.clip(strengthened(array, jax.random.fold_in(own_key, 3), *heavy), -reach, reach).astype(kind)


def setup_inputs(seed: int = 0) -> dict:
    key_list = jax.random.split(jax.random.key(seed), 8)
    tokens = gaussian(key_list[0], (TOKENS, D), 1.0, 6.0, ((0, 4), (1, 8)))
    routes_keys = jax.random.split(jax.random.fold_in(key_list[1], 1), TOKENS // TOK_DEV)
    routes_turns = jax.random.permutation(jax.random.fold_in(key_list[1], 3), TOKENS // TOK_DEV)
    routes = jax.vmap(lambda own, number: routed_block(jax.random.fold_in(key_list[1], 2), own, number, TOK_DEV, NEXP, TOP, CAP, 1))(routes_keys, routes_turns).reshape((TOKENS, TOP))
    mix_weights = jnp.clip(0.2 + 0.8 * jax.random.uniform(key_list[2], (TOKENS, TOP), jnp.float32) ** block_scale(key_list[2], (TOKENS, TOP), ((0, 4),), -0.2, 0.2), 0.2, 1.0)
    w_gate = heavy_noise(key_list[3], (NEXP, D, FF), D ** -0.5, 0.125, ((0, 4), (2, 8)), (2, 1, 8, 2.0))
    w_up = heavy_noise(key_list[4], (NEXP, D, FF), D ** -0.5, 0.125, ((0, 4), (2, 8)), (2, 1, 8, 2.0))
    w_down = heavy_noise(key_list[5], (NEXP, FF, D), FF ** -0.5, 0.09375, ((0, 4), (1, 8)), (1, 2, 8, 2.0))
    upstream = gaussian(key_list[6], (TOKENS, D), 1.0, 6.0, ((0, 4), (1, 8)))
    return {"tokens": tokens, "routes": routes, "mix_weights": mix_weights, "w_gate": w_gate, "w_up": w_up, "w_down": w_down, "upstream": upstream}


highest = lax.Precision.HIGHEST


def slot_tables(route_rows, mix_rows, capacity, experts):
    tok_count, top_count = route_rows.shape
    flat_routes = route_rows.reshape(-1)
    onehot = (flat_routes[:, None] == jnp.arange(experts, dtype=jnp.int32)[None, :]).astype(jnp.int32)
    earlier = jnp.cumsum(onehot, axis=0) - onehot
    position = jnp.sum(earlier * onehot, axis=1)
    target = (flat_routes * capacity + position).reshape(tok_count, top_count)
    slot_ids = jnp.arange(experts * capacity, dtype=jnp.int32)
    matches = (target[None, :, :] == slot_ids[:, None, None]).astype(jnp.float32)
    select = jnp.sum(matches, axis=2)
    weighted = jnp.sum(matches * mix_rows[None, :, :], axis=2)
    return target, select, weighted


def group_sum(make_part, shape):
    def step(index, total):
        part = make_part(index).astype(jnp.bfloat16)
        part = lax.optimization_barrier(part)
        return total + part.astype(jnp.float32)
    return lax.fori_loop(0, N_SECTION, step, jnp.zeros(shape, jnp.float32))


def expert_pass(xin, grad_rows, gate_w, up_w, down_w):
    group_width = FF // N_SECTION
    row_count = xin.shape[0]
    act_gate = jnp.dot(xin, gate_w, preferred_element_type=jnp.float32)
    act_up = jnp.dot(xin, up_w, preferred_element_type=jnp.float32)
    sig = jax.nn.sigmoid(act_gate)
    silu_gate = act_gate * sig
    hidden = (silu_gate * act_up).astype(jnp.bfloat16)

    def out_part(index):
        start = index * group_width
        return jnp.dot(lax.dynamic_slice_in_dim(hidden, start, group_width, 1),
                       lax.dynamic_slice_in_dim(down_w, start, group_width, 0),
                       preferred_element_type=jnp.float32)

    expert_out = group_sum(out_part, (row_count, D)).astype(jnp.bfloat16)
    grad_hidden = lax.dot_general(grad_rows, down_w, (((1,), (1,)), ((), ())), preferred_element_type=jnp.float32)
    grad_down = lax.dot_general(hidden, grad_rows, (((0,), (0,)), ((), ())), preferred_element_type=jnp.float32).astype(jnp.bfloat16)
    dsilu = sig * (1.0 + act_gate * (1.0 - sig))
    grad_act_gate = (grad_hidden * act_up * dsilu).astype(jnp.bfloat16)
    grad_act_up = (grad_hidden * silu_gate).astype(jnp.bfloat16)
    grad_gate = lax.dot_general(xin, grad_act_gate, (((0,), (0,)), ((), ())), preferred_element_type=jnp.float32).astype(jnp.bfloat16)
    grad_up = lax.dot_general(xin, grad_act_up, (((0,), (0,)), ((), ())), preferred_element_type=jnp.float32).astype(jnp.bfloat16)

    def back_part(index):
        start = index * group_width
        first = lax.dot_general(lax.dynamic_slice_in_dim(grad_act_gate, start, group_width, 1),
                                lax.dynamic_slice_in_dim(gate_w, start, group_width, 1),
                                (((1,), (1,)), ((), ())), preferred_element_type=jnp.float32)
        second = lax.dot_general(lax.dynamic_slice_in_dim(grad_act_up, start, group_width, 1),
                                 lax.dynamic_slice_in_dim(up_w, start, group_width, 1),
                                 (((1,), (1,)), ((), ())), preferred_element_type=jnp.float32)
        return first + second

    grad_rows_in = group_sum(back_part, (row_count, D)).astype(jnp.bfloat16)
    return expert_out, grad_rows_in, grad_gate, grad_up, grad_down


def reference(tokens, routes, mix_weights, w_gate, w_up, w_down, upstream):
    blocks = N_EXPERT
    token_blocks = tokens.reshape(blocks, TOK_DEV, D)
    upstream_blocks = upstream.reshape(blocks, TOK_DEV, D)
    target, select, weighted = jax.vmap(lambda route_rows, mix_rows: slot_tables(route_rows, mix_rows, CAP, NEXP))(
        routes.reshape(blocks, TOK_DEV, TOP), mix_weights.reshape(blocks, TOK_DEV, TOP))
    sent = jnp.einsum("bst,btd->bsd", select, token_blocks.astype(jnp.float32), precision=highest).astype(jnp.bfloat16)
    grad_sent = jnp.einsum("bst,btd->bsd", weighted, upstream_blocks.astype(jnp.float32), precision=highest).astype(jnp.bfloat16)

    def to_experts(block):
        return block.reshape(blocks, NEXP, CAP, D).transpose(1, 0, 2, 3).reshape(NEXP, blocks * CAP, D)

    def to_sources(rows):
        return rows.reshape(NEXP, blocks, CAP, D).transpose(1, 0, 2, 3).reshape(blocks, NEXP * CAP, D)

    expert_out, grad_rows_in, grad_gate, grad_up, grad_down = lax.map(
        lambda items: expert_pass(*items), (to_experts(sent), to_experts(grad_sent), w_gate, w_up, w_down))
    returned = to_sources(expert_out).astype(jnp.float32)
    moe_out = jnp.einsum("bst,bsd->btd", weighted, returned, precision=highest)
    mixed = (token_blocks.astype(jnp.float32) + moe_out).astype(jnp.bfloat16).reshape(-1, D)
    picked = jax.vmap(lambda rows, index: rows[index])(returned, target)
    grad_mix = jnp.einsum("btkd,btd->btk", picked, upstream_blocks.astype(jnp.float32), precision=highest).reshape(-1, TOP)
    back_rows = to_sources(grad_rows_in).astype(jnp.float32)
    grad_moe = jnp.einsum("bst,bsd->btd", select, back_rows, precision=highest)
    grad_tokens = (upstream_blocks.astype(jnp.float32) + grad_moe).astype(jnp.bfloat16).reshape(-1, D)
    return (mixed, grad_tokens, grad_mix, grad_gate, grad_up, grad_down)
```

```python
import functools
import jax
import jax.numpy as jnp
from jax import lax
from jax.experimental import pallas as pl
from jax.experimental.pallas import tpu as pltpu
from jax.sharding import PartitionSpec as P

highest = lax.Precision.HIGHEST
MESH = pl.DeviceIdType.MESH
VMEM_BYTES = 60 * 1024 * 1024


class Place:
    def __init__(self, sections):
        section, expert = lax.axis_index("section"), lax.axis_index("expert")
        self.sections, self.lines = sections, sections // 2
        self.z, self.x = lax.div(section, 2), lax.rem(section, 2)
        self.y, self.core = lax.div(expert, 2), lax.rem(expert, 2)
        self.expert = expert

    def device(self, x=None, y=None, z=None, core=None):
        x = self.x if x is None else x
        y = self.y if y is None else y
        z = self.z if z is None else z
        core = self.core if core is None else core
        return (2 * z + x, 2 * y + core)

    def block(self, x, y, z, core):
        return (2 * y + core) * self.sections + 2 * z + x

    def greet(self, others):
        barrier = pltpu.get_barrier_semaphore()
        for other in others:
            pl.semaphore_signal(barrier, inc=1, device_id=other, device_id_type=MESH)
        for step in (1, -1):

            @pl.when((self.z + step >= 0) & (self.z + step < self.lines))
            def _():
                pl.semaphore_signal(
                    barrier, inc=1, device_id=self.device(z=self.z + step), device_id_type=MESH
                )

        ends = jnp.where(self.z > 0, 1, 0) + jnp.where(self.z < self.lines - 1, 1, 0)
        pl.semaphore_wait(barrier, len(others) + ends)


def gather_kernel(
    sections, experts, cap, meta_ref, tok_ref, up_ref, x_ref, u_ref, sel_ref, mix_ref,
    tok_all, up_all, meta_all, send_sem, recv_sem, meta_send, meta_recv,
):
    here = Place(sections)
    x, y, z, core, lines = here.x, here.y, here.z, here.core, here.lines
    held = (tok_all, up_all)
    rows, width = tok_ref.shape
    others = [(2 * z + x, lax.rem(here.expert + j, experts)) for j in range(1, experts)]
    here.greet(others + [here.device(x=1 - x)])

    def copy(a, block, link, target):
        return pltpu.make_async_remote_copy(
            src_ref=held[a].at[block],
            dst_ref=held[a].at[block],
            send_sem=send_sem.at[a, block, link],
            recv_sem=recv_sem.at[a, block],
            device_id=target,
            device_id_type=MESH,
        )

    def meta_copy(j):
        return pltpu.make_async_remote_copy(
            src_ref=meta_all.at[here.expert],
            dst_ref=meta_all.at[here.expert],
            send_sem=meta_send.at[j],
            recv_sem=meta_recv.at[here.expert],
            device_id=others[j],
            device_id_type=MESH,
        )

    own = here.block(x, y, z, core)
    tok_all[own] = tok_ref[...]
    up_all[own] = up_ref[...]
    meta_all[here.expert] = meta_ref[...]
    for j in range(experts - 1):
        meta_copy(j).start()
    buddy = here.device(core=1 - core)
    near = (
        (here.device(x=1 - x), here.device(y=1 - y)),
        (here.device(y=1 - y), here.device(x=1 - x)),
    )

    def sends(d, sign, begin, wait):
        zz = z + sign * d

        def along(a, block, step):
            @pl.when((z + step >= 0) & (z + step < lines))
            def _():
                begin(copy(a, block, 0 if step > 0 else 1, here.device(z=z + step)))

        for a in range(2):
            block = here.block(x, y, zz, core)
            if d > 0:
                wait(a, block)
                along(a, block, -sign)
            else:
                along(a, block, 1)
                along(a, block, -1)
            begin(copy(a, block, 2, near[a][0]))
            begin(copy(a, block, 3, near[a][1]))
            begin(copy(a, block, 4, buddy))
        for a in range(2):
            block = here.block(1 - x, y, zz, core) if a == 0 else here.block(x, 1 - y, zz, core)
            wait(a, block)
            begin(copy(a, block, 3, near[a][1]))
            begin(copy(a, block, 4, buddy))

    def last(d, sign, begin, wait):
        zz = z + sign * d
        for a in range(2):
            first = here.block(x, 1 - y, zz, core) if a == 0 else here.block(1 - x, y, zz, core)
            for block in (first, here.block(1 - x, 1 - y, zz, core)):
                wait(a, block)
                begin(copy(a, block, 4, buddy))

    def walk(begin, wait):
        steps = [(d, sign) for d in range(lines) for sign in ((1,) if d == 0 else (1, -1))]
        queue = [(sends, *steps[0])]
        for before, after in zip(steps, steps[1:]):
            queue += [(sends, *after), (last, *before)]
        queue.append((last, *steps[-1]))
        for part, d, sign in queue:
            zz = z + sign * d
            pl.when((zz >= 0) & (zz < lines))(functools.partial(part, d, sign, begin, wait))

    def arrive(a, block):
        copy(a, block, 4, buddy).wait_recv()

    walk(lambda c: c.start(), arrive)

    for j in range(experts - 1):
        source = lax.rem(here.expert + j + 1, experts)
        pltpu.make_async_remote_copy(
            src_ref=meta_all.at[source],
            dst_ref=meta_all.at[source],
            send_sem=meta_send.at[j],
            recv_sem=meta_recv.at[source],
            device_id=others[j],
            device_id_type=MESH,
        ).wait_recv()
    ids = (lax.broadcasted_iota(jnp.int32, (cap, rows), 0) + here.expert * cap).astype(jnp.float32)
    for b in range(experts):
        table = meta_all[b]
        first = jnp.where(ids == table[0:1, :], 1.0, 0.0)
        second = jnp.where(ids == table[1:2, :], 1.0, 0.0)
        sel_ref[b * cap : (b + 1) * cap, :] = (first + second).astype(jnp.bfloat16)
        mix_ref[b * cap : (b + 1) * cap, :] = jnp.sum(
            first * table[2:3, :] + second * table[3:4, :], axis=1, keepdims=True
        )

    @pl.loop(0, sections)
    def _(s):
        for a in range(2):
            for half in range(experts // 2):
                arrive(a, (2 * half + 1 - core) * sections + s)

    @pl.loop(0, sections)
    def _(s):
        columns = pl.ds(pl.multiple_of(s * width, width), width)
        for b in range(experts):
            take = sel_ref[b * cap : (b + 1) * cap, :]
            for source, out in ((tok_all, x_ref), (up_all, u_ref)):
                out[b * cap : (b + 1) * cap, columns] = jnp.dot(
                    take, source[b * sections + s], preferred_element_type=jnp.float32
                ).astype(jnp.bfloat16)

    walk(lambda c: c.wait_send(), lambda a, block: None)
    for j in range(experts - 1):
        meta_copy(j).wait_send()


def gather_rows(meta, tokens, upstream, sections, experts, cap):
    rows, width = tokens.shape
    total = experts * cap
    blocks = sections * experts
    vmem = pl.BlockSpec(memory_space=pltpu.VMEM)
    return pl.pallas_call(
        functools.partial(gather_kernel, sections, experts, cap),
        out_shape=(
            jax.ShapeDtypeStruct((total, width * sections), jnp.bfloat16),
            jax.ShapeDtypeStruct((total, width * sections), jnp.bfloat16),
            jax.ShapeDtypeStruct((total, rows), jnp.bfloat16),
            jax.ShapeDtypeStruct((total, 1), jnp.float32),
        ),
        in_specs=[vmem] * 3,
        out_specs=[vmem] * 4,
        scratch_shapes=[
            pltpu.VMEM((blocks, rows, width), jnp.bfloat16),
            pltpu.VMEM((blocks, rows, width), jnp.bfloat16),
            pltpu.VMEM((experts,) + meta.shape, jnp.float32),
            pltpu.SemaphoreType.DMA((2, blocks, 5)),
            pltpu.SemaphoreType.DMA((2, blocks)),
            pltpu.SemaphoreType.DMA((experts,)),
            pltpu.SemaphoreType.DMA((experts,)),
        ],
        compiler_params=pltpu.CompilerParams(
            collective_id=0, has_side_effects=True, vmem_limit_bytes=VMEM_BYTES
        ),
        name="gather_rows",
    )(meta, tokens, upstream)


def return_kernel(
    sections, experts, cap, y_ref, z_ref, sel_ref, dot_ref, tok_ref, up_ref,
    mixed_ref, gtok_ref, gmix_ref,
    out, mate, acc, got1, got2, got_up, got_down, tab_out, tab_in,
    mate_s, mate_r, one_s, one_r, two_s, two_r, up_s, up_r, down_s, down_r, tab_s, tab_r,
):
    here = Place(sections)
    x, y, z, core, lines = here.x, here.y, here.z, here.core, here.lines
    rows, width = tok_ref.shape
    parts = (y_ref, z_ref)
    buddy = here.device(core=1 - core)
    partners = [buddy, here.device(x=1 - x), here.device(y=1 - y)]
    far, reach = [], 1
    while reach < lines:
        swapped = z + reach - 2 * reach * lax.rem(lax.div(z, reach), 2)
        partners.append(here.device(z=swapped))
        if reach > 1:
            far.append(here.device(z=swapped))
        reach *= 2
    here.greet(partners[:3] + far)

    def remote(src, dst, send, recv, target):
        return pltpu.make_async_remote_copy(
            src_ref=src, dst_ref=dst, send_sem=send, recv_sem=recv, device_id=target,
            device_id_type=MESH,
        )

    def flip(value, turned):
        return 1 - value if turned else value

    def number(fx, fy, zz):
        return flip(y, fy) * sections + 2 * zz + flip(x, fx)

    def to_tokens(a, fx, fy, zz, which):
        b = 2 * flip(y, fy) + which
        at = pl.ds(pl.multiple_of(b * cap, 16), cap)
        columns = pl.ds(pl.multiple_of((2 * zz + flip(x, fx)) * width, width), width)
        return lax.dot_general(
            sel_ref[at, :], parts[a][at, columns], (((0,), (0,)), ((), ())),
            preferred_element_type=jnp.float32,
        )

    def to_mate(a, fx, fy, zz):
        q = number(fx, fy, zz)
        return remote(out.at[a, q], mate.at[a, q], mate_s.at[a, q], mate_r.at[a, q], buddy)

    def to_first(a, fx, fy, zz):
        q = number(fx, fy, zz)
        slot = (flip(x, fx) if a == 0 else flip(y, fy)) * lines + zz
        target = here.device(y=1 - y) if a == 0 else here.device(x=1 - x)
        return remote(acc.at[a, q], got1.at[a, slot], one_s.at[a, slot], one_r.at[a, slot], target)

    def to_second(a, fx, fy, zz):
        q = number(fx, fy, zz)
        target = here.device(x=1 - x) if a == 0 else here.device(y=1 - y)
        return remote(acc.at[a, q], got2.at[a, zz], two_s.at[a, zz], two_r.at[a, zz], target)

    def to_up(a, zz):
        return remote(
            acc.at[a, number(0, 0, zz)], got_up.at[a, zz], up_s.at[a, zz], up_r.at[a, zz],
            here.device(z=z + 1),
        )

    def to_down(a, zz):
        return remote(
            acc.at[a, number(0, 0, zz)], got_down.at[a, zz], down_s.at[a, zz], down_r.at[a, zz],
            here.device(z=z - 1),
        )

    def add(a, q, *terms):
        value = acc[a, q].astype(jnp.float32)
        for term in terms:
            value = value + term.astype(jnp.float32)
        acc[a, q] = value.astype(jnp.bfloat16)

    def table_copy(i):
        return remote(tab_out.at[i], tab_in.at[i], tab_s.at[i], tab_r.at[i], partners[i])

    def table_step(i):
        table_copy(i).wait_recv()
        tab_out[i + 1] = tab_out[i] + tab_in[i]
        if i + 1 < len(partners):
            table_copy(i + 1).start()

    line = lax.broadcasted_iota(jnp.int32, (8, rows), 0)
    for b in range(experts):
        at = slice(b * cap, (b + 1) * cap)
        sums = jnp.sum(sel_ref[at, :].astype(jnp.float32) * dot_ref[at, :], axis=0, keepdims=True)
        tab_out[0, b] = jnp.where(line == here.expert, sums, 0.0)
    table_copy(0).start()

    def offer(fx, fy):
        @pl.loop(0, lines)
        def _(zz):
            for a in range(2):
                out[a, number(fx, fy, zz)] = to_tokens(a, fx, fy, zz, 1 - core).astype(jnp.bfloat16)
                to_mate(a, fx, fy, zz).start()

    def join(fx, fy):
        @pl.loop(0, lines)
        def _(zz):
            for a in range(2):
                q = number(fx, fy, zz)
                mine = to_tokens(a, fx, fy, zz, core)
                to_mate(a, fx, fy, zz).wait_recv()
                acc[a, q] = (mine + mate[a, q].astype(jnp.float32)).astype(jnp.bfloat16)
                if fy if a == 0 else fx:
                    to_first(a, fx, fy, zz).start()

    offer(1, 1)
    offer(0, 1)
    join(1, 1)
    offer(1, 0)
    join(0, 1)
    offer(0, 0)
    join(1, 0)
    join(0, 0)
    table_step(0)

    @pl.loop(0, lines)
    def _(zz):
        for a in range(2):
            fx, fy = (1, 0) if a == 0 else (0, 1)
            to_first(a, fx, fy, zz).wait_recv()
            slot = (1 - x if a == 0 else 1 - y) * lines + zz
            add(a, number(fx, fy, zz), got1[a, slot])
            to_second(a, fx, fy, zz).start()

    table_step(1)

    @pl.loop(0, lines)
    def _(zz):
        for a in range(2):
            to_first(a, 0, 0, zz).wait_recv()
            slot = (x if a == 0 else y) * lines + zz
            add(a, number(0, 0, zz), got1[a, slot])

    table_step(2)

    def both(do):
        for up, down in zip(range(lines - 1, 0, -1), range(lines - 1)):

            @pl.when(z < up)
            def _():
                for a in range(2):
                    do(a, up, True)

            @pl.when(z > down)
            def _():
                for a in range(2):
                    do(a, down, False)

    def pass_on(a, zz, rising):
        to_second(a, 0, 0, zz).wait_recv()
        q = number(0, 0, zz)
        add(a, q, got2[a, zz])
        if rising:

            @pl.when(z > 0)
            def _():
                to_up(a, zz).wait_recv()
                add(a, q, got_up[a, zz])

            to_up(a, zz).start()
        else:

            @pl.when(z < lines - 1)
            def _():
                to_down(a, zz).wait_recv()
                add(a, q, got_down[a, zz])

            to_down(a, zz).start()

    both(pass_on)
    for i in range(3, len(partners)):
        table_step(i)
    gmix_ref[...] = tab_out[len(partners), here.expert]

    for a, (base, result) in enumerate(((tok_ref, mixed_ref), (up_ref, gtok_ref))):
        to_second(a, 0, 0, z).wait_recv()
        q = number(0, 0, z)
        add(a, q, got2[a, z])

        @pl.when(z > 0)
        def _():
            to_up(a, z).wait_recv()
            add(a, q, got_up[a, z])

        @pl.when(z < lines - 1)
        def _():
            to_down(a, z).wait_recv()
            add(a, q, got_down[a, z])

        result[...] = (base[...].astype(jnp.float32) + acc[a, q].astype(jnp.float32)).astype(
            jnp.bfloat16
        )

    @pl.loop(0, lines)
    def _(zz):
        for a in range(2):
            for fx in (0, 1):
                for fy in (0, 1):
                    to_mate(a, fx, fy, zz).wait_send()
                    if fy if a == 0 else fx:
                        to_first(a, fx, fy, zz).wait_send()
            to_second(a, 1 - a, a, zz).wait_send()

    both(lambda a, zz, rising: (to_up(a, zz) if rising else to_down(a, zz)).wait_send())
    for i in range(len(partners)):
        table_copy(i).wait_send()


def return_rows(part_y, part_z, select, inner, tokens, upstream, sections, experts, cap):
    rows, width = tokens.shape
    lines, half = sections // 2, sections * experts // 2
    steps = 3 + (lines - 1).bit_length()
    vmem = pl.BlockSpec(memory_space=pltpu.VMEM)
    dma = pltpu.SemaphoreType.DMA

    def blocks(count):
        return pltpu.VMEM((2, count, rows, width), jnp.bfloat16)

    return pl.pallas_call(
        functools.partial(return_kernel, sections, experts, cap),
        out_shape=(
            jax.ShapeDtypeStruct(tokens.shape, jnp.bfloat16),
            jax.ShapeDtypeStruct(tokens.shape, jnp.bfloat16),
            jax.ShapeDtypeStruct((8, rows), jnp.float32),
        ),
        in_specs=[vmem] * 6,
        out_specs=[vmem] * 3,
        scratch_shapes=[
            blocks(half), blocks(half), blocks(half), blocks(sections), blocks(lines),
            blocks(lines), blocks(lines),
            pltpu.VMEM((steps + 1, experts, 8, rows), jnp.float32),
            pltpu.VMEM((steps, experts, 8, rows), jnp.float32),
            dma((2, half)), dma((2, half)), dma((2, sections)), dma((2, sections)),
            dma((2, lines)), dma((2, lines)), dma((2, lines)), dma((2, lines)),
            dma((2, lines)), dma((2, lines)), dma((steps,)), dma((steps,)),
        ],
        compiler_params=pltpu.CompilerParams(
            collective_id=1, has_side_effects=True, vmem_limit_bytes=VMEM_BYTES
        ),
        name="return_rows",
    )(part_y, part_z, select, inner, tokens, upstream)


def slot_targets(route_rows, capacity, experts):
    tok_count, top_count = route_rows.shape
    flat_routes = route_rows.reshape(-1)
    onehot = (flat_routes[:, None] == jnp.arange(experts, dtype=jnp.int32)[None, :]).astype(
        jnp.int32
    )
    earlier = jnp.cumsum(onehot, axis=0) - onehot
    position = jnp.sum(earlier * onehot, axis=1)
    return (flat_routes * capacity + position).reshape(tok_count, top_count)


def across(a, b):
    return lax.dot_general(a, b, (((1,), (1,)), ((), ())), preferred_element_type=jnp.float32)


def down(a, b):
    return lax.dot_general(
        a, b, (((0,), (0,)), ((), ())), preferred_element_type=jnp.float32
    ).astype(jnp.bfloat16)


def by_tokens(tokens, routes, mix_weights, w_gate, w_up, w_down, upstream):
    experts, sections = lax.axis_size("expert"), lax.axis_size("section")
    tok_count, top_count = routes.shape
    capacity = 5 * tok_count * top_count // (4 * experts)
    target = slot_targets(routes, capacity, experts)
    meta = jnp.concatenate(
        [target.T.astype(jnp.float32), mix_weights.T, jnp.zeros((4, tok_count), jnp.float32)]
    )
    rows_in, rows_up, select, scale = gather_rows(
        meta, tokens, upstream, sections, experts, capacity
    )
    gate_local, up_local, down_local = w_gate[0], w_up[0], w_down[0]
    act_gate = jnp.dot(rows_in, gate_local, preferred_element_type=jnp.float32)
    act_up = jnp.dot(rows_in, up_local, preferred_element_type=jnp.float32)
    raw = across(rows_up, down_local)
    sig = jax.nn.sigmoid(act_gate)
    silu_gate = act_gate * sig
    hidden = silu_gate * act_up
    inner = jnp.sum(hidden * raw, axis=1, keepdims=True)
    hidden = (hidden * scale).astype(jnp.bfloat16)
    grad_hidden = raw * scale
    dsilu = sig * (1.0 + act_gate * (1.0 - sig))
    grad_act_gate = (grad_hidden * act_up * dsilu).astype(jnp.bfloat16)
    grad_act_up = (grad_hidden * silu_gate).astype(jnp.bfloat16)
    part_y = jnp.dot(hidden, down_local, preferred_element_type=jnp.float32).astype(jnp.bfloat16)
    part_z = (across(grad_act_gate, gate_local) + across(grad_act_up, up_local)).astype(
        jnp.bfloat16
    )
    grad_down = down(hidden, rows_up)
    grad_gate = down(rows_in, grad_act_gate)
    grad_up = down(rows_in, grad_act_up)
    mixed, grad_tokens, table = return_rows(
        part_y, part_z, select, inner, tokens, upstream, sections, experts, capacity
    )
    chosen = routes[:, :, None] == jnp.arange(experts, dtype=jnp.int32)
    grad_mix = jnp.sum(jnp.where(chosen, table[:experts].T[:, None, :], 0.0), axis=2)
    return (mixed, grad_tokens, grad_mix, grad_gate[None], grad_up[None], grad_down[None])


def slot_tables(route_rows, mix_rows, capacity, experts):
    tok_count, top_count = route_rows.shape
    flat_routes = route_rows.reshape(-1)
    onehot = (flat_routes[:, None] == jnp.arange(experts, dtype=jnp.int32)[None, :]).astype(
        jnp.int32
    )
    earlier = jnp.cumsum(onehot, axis=0) - onehot
    position = jnp.sum(earlier * onehot, axis=1)
    target = (flat_routes * capacity + position).reshape(tok_count, top_count)
    slot_ids = jnp.arange(experts * capacity, dtype=jnp.int32)
    hits = target[None, :, :] == slot_ids[:, None, None]
    matches = hits.astype(jnp.float32)
    select = jnp.sum(matches, axis=2)
    weighted = jnp.sum(matches * mix_rows[None, :, :], axis=2)
    token_ids = jnp.arange(tok_count, dtype=jnp.int32)
    slot_token = jnp.sum(jnp.sum(hits.astype(jnp.int32), axis=2) * token_ids[None, :], axis=1)
    return (target, select, weighted, slot_token)


def by_slots(tokens, routes, mix_weights, w_gate, w_up, w_down, upstream):
    experts = lax.axis_size("expert")
    tok_count = tokens.shape[0]
    top_count = routes.shape[1]
    capacity = 5 * tok_count * top_count // (4 * experts)
    slot_total = experts * capacity
    target, select, weighted, slot_token = slot_tables(routes, mix_weights, capacity, experts)
    slot_fill = jnp.sum(select, axis=1)
    slot_scale = jnp.sum(weighted, axis=1)
    gate_local = w_gate[0]
    up_local = w_up[0]
    down_local = w_down[0]

    def collect(source, factor):
        taken = source[slot_token].astype(jnp.float32)
        return (taken * factor[:, None]).astype(jnp.bfloat16)

    def to_experts(source, factor):
        block = collect(source, factor)
        arrived = lax.all_to_all(
            block.reshape(experts, capacity, -1), "expert", split_axis=0, concat_axis=0, tiled=True
        )
        whole = lax.all_gather(arrived, "section", axis=2, tiled=True)
        return whole.reshape(slot_total, -1)

    def to_sources(partial_value):
        summed = lax.psum_scatter(
            partial_value.reshape(experts, capacity, -1).astype(jnp.bfloat16),
            "section",
            scatter_dimension=2,
            tiled=True,
        )
        back = lax.all_to_all(summed, "expert", split_axis=0, concat_axis=0, tiled=True)
        return back.reshape(slot_total, -1)

    dispatched = to_experts(tokens, slot_fill)
    act_gate = jnp.dot(dispatched, gate_local, preferred_element_type=jnp.float32)
    act_up = jnp.dot(dispatched, up_local, preferred_element_type=jnp.float32)
    sig = jax.nn.sigmoid(act_gate)
    silu_gate = act_gate * sig
    hidden = (silu_gate * act_up).astype(jnp.bfloat16)
    partial_value = jnp.dot(hidden, down_local, preferred_element_type=jnp.float32)
    returned = to_sources(partial_value).astype(jnp.float32)
    moe_out = jnp.dot(weighted.T, returned, precision=highest)
    mixed = (tokens.astype(jnp.float32) + moe_out).astype(jnp.bfloat16)
    picked = returned[target]
    upstream_wide = upstream.astype(jnp.float32)
    mix_terms = jnp.einsum("tkd,td->tk", picked, upstream_wide, precision=highest)
    grad_mix = lax.psum(mix_terms, "section")
    grad_rows = to_experts(upstream, slot_scale)
    grad_hidden = lax.dot_general(
        grad_rows, down_local, (((1,), (1,)), ((), ())), preferred_element_type=jnp.float32
    )
    grad_down = lax.dot_general(
        hidden, grad_rows, (((0,), (0,)), ((), ())), preferred_element_type=jnp.float32
    ).astype(jnp.bfloat16)
    dsilu = sig * (1.0 + act_gate * (1.0 - sig))
    grad_act_gate = (grad_hidden * act_up * dsilu).astype(jnp.bfloat16)
    grad_act_up = (grad_hidden * silu_gate).astype(jnp.bfloat16)
    grad_gate = lax.dot_general(
        dispatched, grad_act_gate, (((0,), (0,)), ((), ())), preferred_element_type=jnp.float32
    ).astype(jnp.bfloat16)
    grad_up = lax.dot_general(
        dispatched, grad_act_up, (((0,), (0,)), ((), ())), preferred_element_type=jnp.float32
    ).astype(jnp.bfloat16)
    first = lax.dot_general(
        grad_act_gate, gate_local, (((1,), (1,)), ((), ())), preferred_element_type=jnp.float32
    )
    second = lax.dot_general(
        grad_act_up, up_local, (((1,), (1,)), ((), ())), preferred_element_type=jnp.float32
    )
    back_rows = to_sources(first + second).astype(jnp.float32)
    grad_moe = jnp.dot(select.T, back_rows, precision=highest)
    grad_tokens = (upstream_wide + grad_moe).astype(jnp.bfloat16)
    return (mixed, grad_tokens, grad_mix, grad_gate[None], grad_up[None], grad_down[None])


def per_device(*arrays):
    tokens, routes = arrays[:2]
    experts = lax.axis_size("expert")
    slots = 5 * tokens.shape[0] * routes.shape[1] // 4
    if experts * tokens.shape[0] <= 2 * slots:
        return by_tokens(*arrays)
    return by_slots(*arrays)


def solution(mesh):
    return jax.shard_map(
        per_device,
        mesh=mesh,
        in_specs=(
            P("expert", "section"),
            P("expert", None),
            P("expert", None),
            P("expert", None, "section"),
            P("expert", None, "section"),
            P("expert", "section", None),
            P("expert", "section"),
        ),
        out_specs=(
            P("expert", "section"),
            P("expert", "section"),
            P("expert", None),
            P("expert", None, "section"),
            P("expert", None, "section"),
            P("expert", "section", None),
        ),
        check_vma=False,
    )
```

```python
import functools
import jax
import jax.numpy as jnp
from jax import lax
from jax.experimental import pallas as pl
from jax.experimental.pallas import tpu as pltpu
from jax.sharding import PartitionSpec as P

highest = lax.Precision.HIGHEST
MESH = pl.DeviceIdType.MESH
VMEM_BYTES = 60 * 1024 * 1024


class Place:
    def __init__(self, sections):
        section, expert = lax.axis_index("section"), lax.axis_index("expert")
        self.sections, self.lines = sections, sections // 2
        self.z, self.x = lax.div(section, 2), lax.rem(section, 2)
        self.y, self.core = lax.div(expert, 2), lax.rem(expert, 2)
        self.expert = expert

    def device(self, x=None, y=None, z=None, core=None):
        x = self.x if x is None else x
        y = self.y if y is None else y
        z = self.z if z is None else z
        core = self.core if core is None else core
        return (2 * z + x, 2 * y + core)

    def block(self, x, y, z, core):
        return (2 * y + core) * self.sections + 2 * z + x

    def greet(self, others):
        barrier = pltpu.get_barrier_semaphore()
        for other in others:
            pl.semaphore_signal(barrier, inc=1, device_id=other, device_id_type=MESH)
        for step in (1, -1):

            @pl.when((self.z + step >= 0) & (self.z + step < self.lines))
            def _():
                pl.semaphore_signal(
                    barrier, inc=1, device_id=self.device(z=self.z + step), device_id_type=MESH
                )

        ends = jnp.where(self.z > 0, 1, 0) + jnp.where(self.z < self.lines - 1, 1, 0)
        pl.semaphore_wait(barrier, len(others) + ends)


def gather_kernel(
    sections, experts, cap, meta_ref, tok_ref, up_ref, x_ref, u_ref, sel_ref, mix_ref,
    tok_all, up_all, meta_all, send_sem, recv_sem, meta_send, meta_recv,
):
    here = Place(sections)
    x, y, z, core, lines = here.x, here.y, here.z, here.core, here.lines
    held = (tok_all, up_all)
    rows, width = tok_ref.shape
    others = [(2 * z + x, lax.rem(here.expert + j, experts)) for j in range(1, experts)]
    here.greet(others + [here.device(x=1 - x)])

    def copy(a, block, link, target):
        return pltpu.make_async_remote_copy(
            src_ref=held[a].at[block],
            dst_ref=held[a].at[block],
            send_sem=send_sem.at[a, block, link],
            recv_sem=recv_sem.at[a, block],
            device_id=target,
            device_id_type=MESH,
        )

    def meta_copy(j):
        return pltpu.make_async_remote_copy(
            src_ref=meta_all.at[here.expert],
            dst_ref=meta_all.at[here.expert],
            send_sem=meta_send.at[j],
            recv_sem=meta_recv.at[here.expert],
            device_id=others[j],
            device_id_type=MESH,
        )

    own = here.block(x, y, z, core)
    tok_all[own] = tok_ref[...]
    up_all[own] = up_ref[...]
    meta_all[here.expert] = meta_ref[...]
    for j in range(experts - 1):
        meta_copy(j).start()
    buddy = here.device(core=1 - core)
    near = (
        (here.device(x=1 - x), here.device(y=1 - y)),
        (here.device(y=1 - y), here.device(x=1 - x)),
    )

    def sends(d, sign, begin, wait):
        zz = z + sign * d

        def along(a, block, step):
            @pl.when((z + step >= 0) & (z + step < lines))
            def _():
                begin(copy(a, block, 0 if step > 0 else 1, here.device(z=z + step)))

        for a in range(2):
            block = here.block(x, y, zz, core)
            if d > 0:
                wait(a, block)
                along(a, block, -sign)
            else:
                along(a, block, 1)
                along(a, block, -1)
            begin(copy(a, block, 2, near[a][0]))
            begin(copy(a, block, 3, near[a][1]))
            begin(copy(a, block, 4, buddy))
        for a in range(2):
            block = here.block(1 - x, y, zz, core) if a == 0 else here.block(x, 1 - y, zz, core)
            wait(a, block)
            begin(copy(a, block, 3, near[a][1]))
            begin(copy(a, block, 4, buddy))

    def last(d, sign, begin, wait):
        zz = z + sign * d
        for a in range(2):
            first = here.block(x, 1 - y, zz, core) if a == 0 else here.block(1 - x, y, zz, core)
            for block in (first, here.block(1 - x, 1 - y, zz, core)):
                wait(a, block)
                begin(copy(a, block, 4, buddy))

    def walk(begin, wait):
        steps = [(d, sign) for d in range(lines) for sign in ((1,) if d == 0 else (1, -1))]
        queue = [(sends, *steps[0])]
        for before, after in zip(steps, steps[1:]):
            queue += [(sends, *after), (last, *before)]
        queue.append((last, *steps[-1]))
        for part, d, sign in queue:
            zz = z + sign * d
            pl.when((zz >= 0) & (zz < lines))(functools.partial(part, d, sign, begin, wait))

    def arrive(a, block):
        copy(a, block, 4, buddy).wait_recv()

    walk(lambda c: c.start(), arrive)

    for j in range(experts - 1):
        source = lax.rem(here.expert + j + 1, experts)
        pltpu.make_async_remote_copy(
            src_ref=meta_all.at[source],
            dst_ref=meta_all.at[source],
            send_sem=meta_send.at[j],
            recv_sem=meta_recv.at[source],
            device_id=others[j],
            device_id_type=MESH,
        ).wait_recv()
    ids = (lax.broadcasted_iota(jnp.int32, (cap, rows), 0) + here.expert * cap).astype(jnp.float32)
    for b in range(experts):
        table = meta_all[b]
        first = jnp.where(ids == table[0:1, :], 1.0, 0.0)
        second = jnp.where(ids == table[1:2, :], 1.0, 0.0)
        sel_ref[b * cap : (b + 1) * cap, :] = (first + second).astype(jnp.bfloat16)
        mix_ref[b * cap : (b + 1) * cap, :] = jnp.sum(
            first * table[2:3, :] + second * table[3:4, :], axis=1, keepdims=True
        )

    def dispatch(s, which):
        columns = pl.ds(pl.multiple_of(s * width, width), width)
        for half in range(experts // 2):
            b = 2 * half + which
            at = pl.ds(pl.multiple_of(b * cap, 16), cap)
            for a, out in enumerate((x_ref, u_ref)):
                out[at, columns] = jnp.dot(
                    sel_ref[at, :], held[a][b * sections + s], preferred_element_type=jnp.float32
                ).astype(jnp.bfloat16)

    @pl.loop(0, sections)
    def _(s):
        dispatch(s, core)

    @pl.loop(0, sections)
    def _(s):
        for a in range(2):
            for half in range(experts // 2):
                arrive(a, (2 * half + 1 - core) * sections + s)
        dispatch(s, 1 - core)

    walk(lambda c: c.wait_send(), lambda a, block: None)
    for j in range(experts - 1):
        meta_copy(j).wait_send()


def gather_rows(meta, tokens, upstream, sections, experts, cap):
    rows, width = tokens.shape
    total = experts * cap
    blocks = sections * experts
    vmem = pl.BlockSpec(memory_space=pltpu.VMEM)
    return pl.pallas_call(
        functools.partial(gather_kernel, sections, experts, cap),
        out_shape=(
            jax.ShapeDtypeStruct((total, width * sections), jnp.bfloat16),
            jax.ShapeDtypeStruct((total, width * sections), jnp.bfloat16),
            jax.ShapeDtypeStruct((total, rows), jnp.bfloat16),
            jax.ShapeDtypeStruct((total, 1), jnp.float32),
        ),
        in_specs=[vmem] * 3,
        out_specs=[vmem] * 4,
        scratch_shapes=[
            pltpu.VMEM((blocks, rows, width), jnp.bfloat16),
            pltpu.VMEM((blocks, rows, width), jnp.bfloat16),
            pltpu.VMEM((experts,) + meta.shape, jnp.float32),
            pltpu.SemaphoreType.DMA((2, blocks, 5)),
            pltpu.SemaphoreType.DMA((2, blocks)),
            pltpu.SemaphoreType.DMA((experts,)),
            pltpu.SemaphoreType.DMA((experts,)),
        ],
        compiler_params=pltpu.CompilerParams(
            collective_id=0, has_side_effects=True, vmem_limit_bytes=VMEM_BYTES
        ),
        name="gather_rows",
    )(meta, tokens, upstream)


def return_kernel(
    sections, experts, cap, y_ref, z_ref, sel_ref, dot_ref, tok_ref, up_ref,
    mixed_ref, gtok_ref, gmix_ref,
    out, mate, acc, got1, got2, got_up, got_down, tab_out, tab_in,
    mate_s, mate_r, one_s, one_r, two_s, two_r, up_s, up_r, down_s, down_r, tab_s, tab_r,
):
    here = Place(sections)
    x, y, z, core, lines = here.x, here.y, here.z, here.core, here.lines
    rows, width = tok_ref.shape
    parts = (y_ref, z_ref)
    buddy = here.device(core=1 - core)
    partners = [buddy, here.device(x=1 - x), here.device(y=1 - y)]
    far, reach = [], 1
    while reach < lines:
        swapped = z + reach - 2 * reach * lax.rem(lax.div(z, reach), 2)
        partners.append(here.device(z=swapped))
        if reach > 1:
            far.append(here.device(z=swapped))
        reach *= 2
    here.greet(partners[:3] + far)

    def remote(src, dst, send, recv, target):
        return pltpu.make_async_remote_copy(
            src_ref=src, dst_ref=dst, send_sem=send, recv_sem=recv, device_id=target,
            device_id_type=MESH,
        )

    def flip(value, turned):
        return 1 - value if turned else value

    def number(fx, fy, zz):
        return flip(y, fy) * sections + 2 * zz + flip(x, fx)

    def to_tokens(a, fx, fy, zz, which):
        b = 2 * flip(y, fy) + which
        at = pl.ds(pl.multiple_of(b * cap, 16), cap)
        columns = pl.ds(pl.multiple_of((2 * zz + flip(x, fx)) * width, width), width)
        return lax.dot_general(
            sel_ref[at, :], parts[a][at, columns], (((0,), (0,)), ((), ())),
            preferred_element_type=jnp.float32,
        )

    def to_mate(a, fx, fy, zz):
        q = number(fx, fy, zz)
        return remote(out.at[a, q], mate.at[a, q], mate_s.at[a, q], mate_r.at[a, q], buddy)

    def to_first(a, fx, fy, zz):
        q = number(fx, fy, zz)
        slot = (flip(x, fx) if a == 0 else flip(y, fy)) * lines + zz
        target = here.device(y=1 - y) if a == 0 else here.device(x=1 - x)
        return remote(acc.at[a, q], got1.at[a, slot], one_s.at[a, slot], one_r.at[a, slot], target)

    def to_second(a, fx, fy, zz):
        q = number(fx, fy, zz)
        target = here.device(x=1 - x) if a == 0 else here.device(y=1 - y)
        return remote(acc.at[a, q], got2.at[a, zz], two_s.at[a, zz], two_r.at[a, zz], target)

    def to_up(a, zz):
        return remote(
            acc.at[a, number(0, 0, zz)], got_up.at[a, zz], up_s.at[a, zz], up_r.at[a, zz],
            here.device(z=z + 1),
        )

    def to_down(a, zz):
        return remote(
            acc.at[a, number(0, 0, zz)], got_down.at[a, zz], down_s.at[a, zz], down_r.at[a, zz],
            here.device(z=z - 1),
        )

    def add(a, q, *terms):
        value = acc[a, q].astype(jnp.float32)
        for term in terms:
            value = value + term.astype(jnp.float32)
        acc[a, q] = value.astype(jnp.bfloat16)

    def table_copy(i):
        return remote(tab_out.at[i], tab_in.at[i], tab_s.at[i], tab_r.at[i], partners[i])

    def table_step(i):
        table_copy(i).wait_recv()
        tab_out[i + 1] = tab_out[i] + tab_in[i]
        if i + 1 < len(partners):
            table_copy(i + 1).start()

    line = lax.broadcasted_iota(jnp.int32, (8, rows), 0)
    for b in range(experts):
        at = slice(b * cap, (b + 1) * cap)
        sums = jnp.sum(sel_ref[at, :].astype(jnp.float32) * dot_ref[at, :], axis=0, keepdims=True)
        tab_out[0, b] = jnp.where(line == here.expert, sums, 0.0)
    table_copy(0).start()

    def ends_first(i):
        return lax.div(i, 2) + lax.rem(i, 2) * (lines - 1 - 2 * lax.div(i, 2))

    def offer(fx, fy):
        @pl.loop(0, lines)
        def _(i):
            zz = ends_first(i)
            for a in range(2):
                out[a, number(fx, fy, zz)] = to_tokens(a, fx, fy, zz, 1 - core).astype(jnp.bfloat16)
                to_mate(a, fx, fy, zz).start()

    def join(fx, fy):
        @pl.loop(0, lines)
        def _(i):
            zz = ends_first(i)
            for a in range(2):
                q = number(fx, fy, zz)
                mine = to_tokens(a, fx, fy, zz, core)
                to_mate(a, fx, fy, zz).wait_recv()
                acc[a, q] = (mine + mate[a, q].astype(jnp.float32)).astype(jnp.bfloat16)
                if fy if a == 0 else fx:
                    to_first(a, fx, fy, zz).start()

    offer(1, 1)
    table_step(0)
    offer(0, 1)
    table_step(1)
    join(1, 1)
    table_step(2)
    offer(1, 0)
    join(0, 1)
    offer(0, 0)
    join(1, 0)
    join(0, 0)
    for i in range(3, len(partners)):
        table_step(i)

    @pl.loop(0, lines)
    def _(i):
        zz = ends_first(i)
        for a in range(2):
            fx, fy = (1, 0) if a == 0 else (0, 1)
            to_first(a, fx, fy, zz).wait_recv()
            slot = (1 - x if a == 0 else 1 - y) * lines + zz
            add(a, number(fx, fy, zz), got1[a, slot])
            to_second(a, fx, fy, zz).start()

    @pl.loop(0, lines)
    def _(zz):
        for a in range(2):
            to_first(a, 0, 0, zz).wait_recv()
            slot = (x if a == 0 else y) * lines + zz
            add(a, number(0, 0, zz), got1[a, slot])

    def both(do):
        for up, down in zip(range(lines - 1, 0, -1), range(lines - 1)):

            @pl.when(z < up)
            def _():
                for a in range(2):
                    do(a, up, True)

            @pl.when(z > down)
            def _():
                for a in range(2):
                    do(a, down, False)

    def pass_on(a, zz, rising):
        to_second(a, 0, 0, zz).wait_recv()
        q = number(0, 0, zz)
        add(a, q, got2[a, zz])
        if rising:

            @pl.when(z > 0)
            def _():
                to_up(a, zz).wait_recv()
                add(a, q, got_up[a, zz])

            to_up(a, zz).start()
        else:

            @pl.when(z < lines - 1)
            def _():
                to_down(a, zz).wait_recv()
                add(a, q, got_down[a, zz])

            to_down(a, zz).start()

    both(pass_on)
    gmix_ref[...] = tab_out[len(partners), here.expert]

    for a, (base, result) in enumerate(((tok_ref, mixed_ref), (up_ref, gtok_ref))):
        to_second(a, 0, 0, z).wait_recv()
        q = number(0, 0, z)
        add(a, q, got2[a, z])

        @pl.when(z > 0)
        def _():
            to_up(a, z).wait_recv()
            add(a, q, got_up[a, z])

        @pl.when(z < lines - 1)
        def _():
            to_down(a, z).wait_recv()
            add(a, q, got_down[a, z])

        result[...] = (base[...].astype(jnp.float32) + acc[a, q].astype(jnp.float32)).astype(
            jnp.bfloat16
        )

    @pl.loop(0, lines)
    def _(zz):
        for a in range(2):
            for fx in (0, 1):
                for fy in (0, 1):
                    to_mate(a, fx, fy, zz).wait_send()
                    if fy if a == 0 else fx:
                        to_first(a, fx, fy, zz).wait_send()
            to_second(a, 1 - a, a, zz).wait_send()

    both(lambda a, zz, rising: (to_up(a, zz) if rising else to_down(a, zz)).wait_send())
    for i in range(len(partners)):
        table_copy(i).wait_send()


def return_rows(part_y, part_z, select, inner, tokens, upstream, sections, experts, cap):
    rows, width = tokens.shape
    lines, half = sections // 2, sections * experts // 2
    steps = 3 + (lines - 1).bit_length()
    vmem = pl.BlockSpec(memory_space=pltpu.VMEM)
    dma = pltpu.SemaphoreType.DMA

    def blocks(count):
        return pltpu.VMEM((2, count, rows, width), jnp.bfloat16)

    return pl.pallas_call(
        functools.partial(return_kernel, sections, experts, cap),
        out_shape=(
            jax.ShapeDtypeStruct(tokens.shape, jnp.bfloat16),
            jax.ShapeDtypeStruct(tokens.shape, jnp.bfloat16),
            jax.ShapeDtypeStruct((8, rows), jnp.float32),
        ),
        in_specs=[vmem] * 6,
        out_specs=[vmem] * 3,
        scratch_shapes=[
            blocks(half), blocks(half), blocks(half), blocks(sections), blocks(lines),
            blocks(lines), blocks(lines),
            pltpu.VMEM((steps + 1, experts, 8, rows), jnp.float32),
            pltpu.VMEM((steps, experts, 8, rows), jnp.float32),
            dma((2, half)), dma((2, half)), dma((2, sections)), dma((2, sections)),
            dma((2, lines)), dma((2, lines)), dma((2, lines)), dma((2, lines)),
            dma((2, lines)), dma((2, lines)), dma((steps,)), dma((steps,)),
        ],
        compiler_params=pltpu.CompilerParams(
            collective_id=1, has_side_effects=True, vmem_limit_bytes=VMEM_BYTES
        ),
        name="return_rows",
    )(part_y, part_z, select, inner, tokens, upstream)


def slot_targets(route_rows, capacity, experts):
    tok_count, top_count = route_rows.shape
    flat_routes = route_rows.reshape(-1)
    onehot = (flat_routes[:, None] == jnp.arange(experts, dtype=jnp.int32)[None, :]).astype(
        jnp.int32
    )
    earlier = jnp.cumsum(onehot, axis=0) - onehot
    position = jnp.sum(earlier * onehot, axis=1)
    return (flat_routes * capacity + position).reshape(tok_count, top_count)


def across(a, b):
    return lax.dot_general(a, b, (((1,), (1,)), ((), ())), preferred_element_type=jnp.float32)


def down(a, b):
    return lax.dot_general(
        a, b, (((0,), (0,)), ((), ())), preferred_element_type=jnp.float32
    ).astype(jnp.bfloat16)


def by_tokens(tokens, routes, mix_weights, w_gate, w_up, w_down, upstream):
    experts, sections = lax.axis_size("expert"), lax.axis_size("section")
    tok_count, top_count = routes.shape
    capacity = 5 * tok_count * top_count // (4 * experts)
    target = slot_targets(routes, capacity, experts)
    meta = jnp.concatenate(
        [target.T.astype(jnp.float32), mix_weights.T, jnp.zeros((4, tok_count), jnp.float32)]
    )
    rows_in, rows_up, select, scale = gather_rows(
        meta, tokens, upstream, sections, experts, capacity
    )
    gate_local, up_local, down_local = w_gate[0], w_up[0], w_down[0]
    act_gate = jnp.dot(rows_in, gate_local, preferred_element_type=jnp.float32)
    act_up = jnp.dot(rows_in, up_local, preferred_element_type=jnp.float32)
    raw = across(rows_up, down_local)
    sig = jax.nn.sigmoid(act_gate)
    silu_gate = act_gate * sig
    hidden = silu_gate * act_up
    inner = jnp.sum(hidden * raw, axis=1, keepdims=True)
    hidden = (hidden * scale).astype(jnp.bfloat16)
    grad_hidden = raw * scale
    dsilu = sig * (1.0 + act_gate * (1.0 - sig))
    grad_act_gate = (grad_hidden * act_up * dsilu).astype(jnp.bfloat16)
    grad_act_up = (grad_hidden * silu_gate).astype(jnp.bfloat16)
    part_y = jnp.dot(hidden, down_local, preferred_element_type=jnp.float32).astype(jnp.bfloat16)
    part_z = (across(grad_act_gate, gate_local) + across(grad_act_up, up_local)).astype(
        jnp.bfloat16
    )
    grad_down = down(hidden, rows_up)
    grad_gate = down(rows_in, grad_act_gate)
    grad_up = down(rows_in, grad_act_up)
    mixed, grad_tokens, table = return_rows(
        part_y, part_z, select, inner, tokens, upstream, sections, experts, capacity
    )
    chosen = routes[:, :, None] == jnp.arange(experts, dtype=jnp.int32)
    grad_mix = jnp.sum(jnp.where(chosen, table[:experts].T[:, None, :], 0.0), axis=2)
    return (mixed, grad_tokens, grad_mix, grad_gate[None], grad_up[None], grad_down[None])


def slot_tables(route_rows, mix_rows, capacity, experts):
    tok_count, top_count = route_rows.shape
    flat_routes = route_rows.reshape(-1)
    onehot = (flat_routes[:, None] == jnp.arange(experts, dtype=jnp.int32)[None, :]).astype(
        jnp.int32
    )
    earlier = jnp.cumsum(onehot, axis=0) - onehot
    position = jnp.sum(earlier * onehot, axis=1)
    target = (flat_routes * capacity + position).reshape(tok_count, top_count)
    slot_ids = jnp.arange(experts * capacity, dtype=jnp.int32)
    hits = target[None, :, :] == slot_ids[:, None, None]
    matches = hits.astype(jnp.float32)
    select = jnp.sum(matches, axis=2)
    weighted = jnp.sum(matches * mix_rows[None, :, :], axis=2)
    token_ids = jnp.arange(tok_count, dtype=jnp.int32)
    slot_token = jnp.sum(jnp.sum(hits.astype(jnp.int32), axis=2) * token_ids[None, :], axis=1)
    return (target, select, weighted, slot_token)


def by_slots(tokens, routes, mix_weights, w_gate, w_up, w_down, upstream):
    experts = lax.axis_size("expert")
    tok_count = tokens.shape[0]
    top_count = routes.shape[1]
    capacity = 5 * tok_count * top_count // (4 * experts)
    slot_total = experts * capacity
    target, select, weighted, slot_token = slot_tables(routes, mix_weights, capacity, experts)
    slot_fill = jnp.sum(select, axis=1)
    slot_scale = jnp.sum(weighted, axis=1)
    gate_local = w_gate[0]
    up_local = w_up[0]
    down_local = w_down[0]

    def collect(source, factor):
        taken = source[slot_token].astype(jnp.float32)
        return (taken * factor[:, None]).astype(jnp.bfloat16)

    def to_experts(source, factor):
        block = collect(source, factor)
        arrived = lax.all_to_all(
            block.reshape(experts, capacity, -1), "expert", split_axis=0, concat_axis=0, tiled=True
        )
        whole = lax.all_gather(arrived, "section", axis=2, tiled=True)
        return whole.reshape(slot_total, -1)

    def to_sources(partial_value):
        summed = lax.psum_scatter(
            partial_value.reshape(experts, capacity, -1).astype(jnp.bfloat16),
            "section",
            scatter_dimension=2,
            tiled=True,
        )
        back = lax.all_to_all(summed, "expert", split_axis=0, concat_axis=0, tiled=True)
        return back.reshape(slot_total, -1)

    dispatched = to_experts(tokens, slot_fill)
    act_gate = jnp.dot(dispatched, gate_local, preferred_element_type=jnp.float32)
    act_up = jnp.dot(dispatched, up_local, preferred_element_type=jnp.float32)
    sig = jax.nn.sigmoid(act_gate)
    silu_gate = act_gate * sig
    hidden = (silu_gate * act_up).astype(jnp.bfloat16)
    partial_value = jnp.dot(hidden, down_local, preferred_element_type=jnp.float32)
    returned = to_sources(partial_value).astype(jnp.float32)
    moe_out = jnp.dot(weighted.T, returned, precision=highest)
    mixed = (tokens.astype(jnp.float32) + moe_out).astype(jnp.bfloat16)
    picked = returned[target]
    upstream_wide = upstream.astype(jnp.float32)
    mix_terms = jnp.einsum("tkd,td->tk", picked, upstream_wide, precision=highest)
    grad_mix = lax.psum(mix_terms, "section")
    grad_rows = to_experts(upstream, slot_scale)
    grad_hidden = lax.dot_general(
        grad_rows, down_local, (((1,), (1,)), ((), ())), preferred_element_type=jnp.float32
    )
    grad_down = lax.dot_general(
        hidden, grad_rows, (((0,), (0,)), ((), ())), preferred_element_type=jnp.float32
    ).astype(jnp.bfloat16)
    dsilu = sig * (1.0 + act_gate * (1.0 - sig))
    grad_act_gate = (grad_hidden * act_up * dsilu).astype(jnp.bfloat16)
    grad_act_up = (grad_hidden * silu_gate).astype(jnp.bfloat16)
    grad_gate = lax.dot_general(
        dispatched, grad_act_gate, (((0,), (0,)), ((), ())), preferred_element_type=jnp.float32
    ).astype(jnp.bfloat16)
    grad_up = lax.dot_general(
        dispatched, grad_act_up, (((0,), (0,)), ((), ())), preferred_element_type=jnp.float32
    ).astype(jnp.bfloat16)
    first = lax.dot_general(
        grad_act_gate, gate_local, (((1,), (1,)), ((), ())), preferred_element_type=jnp.float32
    )
    second = lax.dot_general(
        grad_act_up, up_local, (((1,), (1,)), ((), ())), preferred_element_type=jnp.float32
    )
    back_rows = to_sources(first + second).astype(jnp.float32)
    grad_moe = jnp.dot(select.T, back_rows, precision=highest)
    grad_tokens = (upstream_wide + grad_moe).astype(jnp.bfloat16)
    return (mixed, grad_tokens, grad_mix, grad_gate[None], grad_up[None], grad_down[None])


def per_device(*arrays):
    tokens, routes = arrays[:2]
    experts = lax.axis_size("expert")
    slots = 5 * tokens.shape[0] * routes.shape[1] // 4
    if experts * tokens.shape[0] <= 2 * slots:
        return by_tokens(*arrays)
    return by_slots(*arrays)


def solution(mesh):
    return jax.shard_map(
        per_device,
        mesh=mesh,
        in_specs=(
            P("expert", "section"),
            P("expert", None),
            P("expert", None),
            P("expert", None, "section"),
            P("expert", None, "section"),
            P("expert", "section", None),
            P("expert", "section"),
        ),
        out_specs=(
            P("expert", "section"),
            P("expert", "section"),
            P("expert", None),
            P("expert", None, "section"),
            P("expert", None, "section"),
            P("expert", "section", None),
        ),
        check_vma=False,
    )
```

```python
import functools
import jax
import jax.numpy as jnp
from jax import lax
from jax.experimental import pallas as pl
from jax.experimental.pallas import tpu as pltpu
from jax.sharding import PartitionSpec as P

highest = lax.Precision.HIGHEST
MESH = pl.DeviceIdType.MESH
VMEM_BYTES = 60 * 1024 * 1024


class Place:
    def __init__(self, sections):
        section, expert = lax.axis_index("section"), lax.axis_index("expert")
        self.sections, self.lines = sections, sections // 2
        self.z, self.x = lax.div(section, 2), lax.rem(section, 2)
        self.y, self.core = lax.div(expert, 2), lax.rem(expert, 2)
        self.expert = expert

    def device(self, x=None, y=None, z=None, core=None):
        x = self.x if x is None else x
        y = self.y if y is None else y
        z = self.z if z is None else z
        core = self.core if core is None else core
        return (2 * z + x, 2 * y + core)

    def block(self, x, y, z, core):
        return (2 * y + core) * self.sections + 2 * z + x

    def greet(self, others):
        barrier = pltpu.get_barrier_semaphore()
        for other in others:
            pl.semaphore_signal(barrier, inc=1, device_id=other, device_id_type=MESH)
        for step in (1, -1):

            @pl.when((self.z + step >= 0) & (self.z + step < self.lines))
            def _():
                pl.semaphore_signal(
                    barrier, inc=1, device_id=self.device(z=self.z + step), device_id_type=MESH
                )

        ends = jnp.where(self.z > 0, 1, 0) + jnp.where(self.z < self.lines - 1, 1, 0)
        pl.semaphore_wait(barrier, len(others) + ends)


def gather_kernel(
    sections, experts, cap, meta_ref, tok_ref, up_ref, x_ref, u_ref, sel_ref, mix_ref,
    tok_all, up_all, meta_all, send_sem, recv_sem, meta_send, meta_recv,
):
    here = Place(sections)
    x, y, z, core, lines = here.x, here.y, here.z, here.core, here.lines
    held = (tok_all, up_all)
    rows, width = tok_ref.shape
    others = [(2 * z + x, lax.rem(here.expert + j, experts)) for j in range(1, experts)]
    here.greet(others + [here.device(x=1 - x)])

    def copy(a, block, link, target):
        return pltpu.make_async_remote_copy(
            src_ref=held[a].at[block],
            dst_ref=held[a].at[block],
            send_sem=send_sem.at[a, block, link],
            recv_sem=recv_sem.at[a, block],
            device_id=target,
            device_id_type=MESH,
        )

    def meta_copy(j):
        return pltpu.make_async_remote_copy(
            src_ref=meta_all.at[here.expert],
            dst_ref=meta_all.at[here.expert],
            send_sem=meta_send.at[j],
            recv_sem=meta_recv.at[here.expert],
            device_id=others[j],
            device_id_type=MESH,
        )

    own = here.block(x, y, z, core)
    tok_all[own] = tok_ref[...]
    up_all[own] = up_ref[...]
    meta_all[here.expert] = meta_ref[...]
    for j in range(experts - 1):
        meta_copy(j).start()
    buddy = here.device(core=1 - core)
    near = (
        (here.device(x=1 - x), here.device(y=1 - y)),
        (here.device(y=1 - y), here.device(x=1 - x)),
    )

    def sends(d, sign, begin, wait):
        zz = z + sign * d

        def along(a, block, step):
            @pl.when((z + step >= 0) & (z + step < lines))
            def _():
                begin(copy(a, block, 0 if step > 0 else 1, here.device(z=z + step)))

        for a in range(2):
            block = here.block(x, y, zz, core)
            if d > 0:
                wait(a, block)
                along(a, block, -sign)
            else:
                along(a, block, 1)
                along(a, block, -1)
            begin(copy(a, block, 2, near[a][0]))
            begin(copy(a, block, 3, near[a][1]))
            begin(copy(a, block, 4, buddy))
        for a in range(2):
            block = here.block(1 - x, y, zz, core) if a == 0 else here.block(x, 1 - y, zz, core)
            wait(a, block)
            begin(copy(a, block, 3, near[a][1]))
            begin(copy(a, block, 4, buddy))

    def last(d, sign, begin, wait):
        zz = z + sign * d
        for a in range(2):
            first = here.block(x, 1 - y, zz, core) if a == 0 else here.block(1 - x, y, zz, core)
            for block in (first, here.block(1 - x, 1 - y, zz, core)):
                wait(a, block)
                begin(copy(a, block, 4, buddy))

    def walk(begin, wait):
        steps = [(d, sign) for d in range(lines) for sign in ((1,) if d == 0 else (1, -1))]
        queue = [(sends, *steps[0])]
        for before, after in zip(steps, steps[1:]):
            queue += [(sends, *after), (last, *before)]
        queue.append((last, *steps[-1]))
        for part, d, sign in queue:
            zz = z + sign * d
            pl.when((zz >= 0) & (zz < lines))(functools.partial(part, d, sign, begin, wait))

    def arrive(a, block):
        copy(a, block, 4, buddy).wait_recv()

    walk(lambda c: c.start(), arrive)

    for j in range(experts - 1):
        source = lax.rem(here.expert + j + 1, experts)
        pltpu.make_async_remote_copy(
            src_ref=meta_all.at[source],
            dst_ref=meta_all.at[source],
            send_sem=meta_send.at[j],
            recv_sem=meta_recv.at[source],
            device_id=others[j],
            device_id_type=MESH,
        ).wait_recv()
    ids = (lax.broadcasted_iota(jnp.int32, (cap, rows), 0) + here.expert * cap).astype(jnp.float32)
    for b in range(experts):
        table = meta_all[b]
        first = jnp.where(ids == table[0:1, :], 1.0, 0.0)
        second = jnp.where(ids == table[1:2, :], 1.0, 0.0)
        sel_ref[b * cap : (b + 1) * cap, :] = (first + second).astype(jnp.bfloat16)
        mix_ref[b * cap : (b + 1) * cap, :] = jnp.sum(
            first * table[2:3, :] + second * table[3:4, :], axis=1, keepdims=True
        )

    def dispatch(s, which):
        columns = pl.ds(pl.multiple_of(s * width, width), width)
        for half in range(experts // 2):
            b = 2 * half + which
            at = pl.ds(pl.multiple_of(b * cap, 16), cap)
            for a, out in enumerate((x_ref, u_ref)):
                out[at, columns] = jnp.dot(
                    sel_ref[at, :], held[a][b * sections + s], preferred_element_type=jnp.float32
                ).astype(jnp.bfloat16)

    @pl.loop(0, sections)
    def _(s):
        dispatch(s, core)

    @pl.loop(0, sections)
    def _(s):
        for a in range(2):
            for half in range(experts // 2):
                arrive(a, (2 * half + 1 - core) * sections + s)
        dispatch(s, 1 - core)

    walk(lambda c: c.wait_send(), lambda a, block: None)
    for j in range(experts - 1):
        meta_copy(j).wait_send()


def gather_rows(meta, tokens, upstream, sections, experts, cap):
    rows, width = tokens.shape
    total = experts * cap
    blocks = sections * experts
    vmem = pl.BlockSpec(memory_space=pltpu.VMEM)
    return pl.pallas_call(
        functools.partial(gather_kernel, sections, experts, cap),
        out_shape=(
            jax.ShapeDtypeStruct((total, width * sections), jnp.bfloat16),
            jax.ShapeDtypeStruct((total, width * sections), jnp.bfloat16),
            jax.ShapeDtypeStruct((total, rows), jnp.bfloat16),
            jax.ShapeDtypeStruct((total, 1), jnp.float32),
        ),
        in_specs=[vmem] * 3,
        out_specs=[vmem] * 4,
        scratch_shapes=[
            pltpu.VMEM((blocks, rows, width), jnp.bfloat16),
            pltpu.VMEM((blocks, rows, width), jnp.bfloat16),
            pltpu.VMEM((experts,) + meta.shape, jnp.float32),
            pltpu.SemaphoreType.DMA((2, blocks, 5)),
            pltpu.SemaphoreType.DMA((2, blocks)),
            pltpu.SemaphoreType.DMA((experts,)),
            pltpu.SemaphoreType.DMA((experts,)),
        ],
        compiler_params=pltpu.CompilerParams(
            collective_id=0, has_side_effects=True, vmem_limit_bytes=VMEM_BYTES
        ),
        name="gather_rows",
    )(meta, tokens, upstream)


def return_kernel(
    sections, experts, cap, y_ref, z_ref, sel_ref, turn_ref, dot_ref, tok_ref, up_ref,
    mixed_ref, gtok_ref, gmix_ref,
    out, mate, acc, got1, got2, got_up, got_down, tab_out, tab_in,
    mate_s, mate_r, one_s, one_r, two_s, two_r, up_s, up_r, down_s, down_r, tab_s, tab_r,
):
    here = Place(sections)
    x, y, z, core, lines = here.x, here.y, here.z, here.core, here.lines
    rows, width = tok_ref.shape
    parts = (y_ref, z_ref)
    buddy = here.device(core=1 - core)
    partners = [buddy, here.device(x=1 - x), here.device(y=1 - y)]
    far, reach = [], 1
    while reach < lines:
        swapped = z + reach - 2 * reach * lax.rem(lax.div(z, reach), 2)
        partners.append(here.device(z=swapped))
        if reach > 1:
            far.append(here.device(z=swapped))
        reach *= 2
    here.greet(partners[:3] + far)

    def remote(src, dst, send, recv, target):
        return pltpu.make_async_remote_copy(
            src_ref=src, dst_ref=dst, send_sem=send, recv_sem=recv, device_id=target,
            device_id_type=MESH,
        )

    def flip(value, turned):
        return 1 - value if turned else value

    def number(fx, fy, zz):
        return flip(y, fy) * sections + 2 * zz + flip(x, fx)

    def to_tokens(a, fx, fy, zz, which):
        b = 2 * flip(y, fy) + which
        at = pl.ds(pl.multiple_of(b * cap, 16), cap)
        columns = pl.ds(pl.multiple_of((2 * zz + flip(x, fx)) * width, width), width)
        return jnp.dot(
            turn_ref[b], parts[a][at, columns], preferred_element_type=jnp.float32
        )

    def to_mate(a, fx, fy, zz):
        q = number(fx, fy, zz)
        return remote(out.at[a, q], mate.at[a, q], mate_s.at[a, q], mate_r.at[a, q], buddy)

    def to_first(a, fx, fy, zz):
        q = number(fx, fy, zz)
        slot = (flip(x, fx) if a == 0 else flip(y, fy)) * lines + zz
        target = here.device(y=1 - y) if a == 0 else here.device(x=1 - x)
        return remote(acc.at[a, q], got1.at[a, slot], one_s.at[a, slot], one_r.at[a, slot], target)

    def to_second(a, fx, fy, zz):
        q = number(fx, fy, zz)
        target = here.device(x=1 - x) if a == 0 else here.device(y=1 - y)
        return remote(acc.at[a, q], got2.at[a, zz], two_s.at[a, zz], two_r.at[a, zz], target)

    def to_up(a, zz):
        return remote(
            acc.at[a, number(0, 0, zz)], got_up.at[a, zz], up_s.at[a, zz], up_r.at[a, zz],
            here.device(z=z + 1),
        )

    def to_down(a, zz):
        return remote(
            acc.at[a, number(0, 0, zz)], got_down.at[a, zz], down_s.at[a, zz], down_r.at[a, zz],
            here.device(z=z - 1),
        )

    def add(a, q, *terms):
        value = acc[a, q].astype(jnp.float32)
        for term in terms:
            value = value + term.astype(jnp.float32)
        acc[a, q] = value.astype(jnp.bfloat16)

    def table_copy(i):
        return remote(tab_out.at[i], tab_in.at[i], tab_s.at[i], tab_r.at[i], partners[i])

    def table_step(i):
        table_copy(i).wait_recv()
        tab_out[i + 1] = tab_out[i] + tab_in[i]
        if i + 1 < len(partners):
            table_copy(i + 1).start()

    line = lax.broadcasted_iota(jnp.int32, (8, rows), 0)
    for b in range(experts):
        at = slice(b * cap, (b + 1) * cap)
        sums = jnp.sum(sel_ref[at, :].astype(jnp.float32) * dot_ref[at, :], axis=0, keepdims=True)
        tab_out[0, b] = jnp.where(line == here.expert, sums, 0.0)
    table_copy(0).start()

    def ends_first(i):
        return lax.div(i, 2) + lax.rem(i, 2) * (lines - 1 - 2 * lax.div(i, 2))

    def offer(fx, fy):
        @pl.loop(0, lines)
        def _(i):
            zz = ends_first(i)
            for a in range(2):
                out[a, number(fx, fy, zz)] = to_tokens(a, fx, fy, zz, 1 - core).astype(jnp.bfloat16)
                to_mate(a, fx, fy, zz).start()

    def join(fx, fy):
        @pl.loop(0, lines)
        def _(i):
            zz = ends_first(i)
            for a in range(2):
                q = number(fx, fy, zz)
                mine = to_tokens(a, fx, fy, zz, core)
                to_mate(a, fx, fy, zz).wait_recv()
                acc[a, q] = (mine + mate[a, q].astype(jnp.float32)).astype(jnp.bfloat16)
                if fy if a == 0 else fx:
                    to_first(a, fx, fy, zz).start()

    offer(1, 1)
    table_step(0)
    offer(0, 1)
    table_step(1)
    join(1, 1)
    table_step(2)
    offer(1, 0)
    join(0, 1)
    offer(0, 0)
    join(1, 0)
    join(0, 0)
    for i in range(3, len(partners)):
        table_step(i)

    @pl.loop(0, lines)
    def _(i):
        zz = ends_first(i)
        for a in range(2):
            fx, fy = (1, 0) if a == 0 else (0, 1)
            to_first(a, fx, fy, zz).wait_recv()
            slot = (1 - x if a == 0 else 1 - y) * lines + zz
            add(a, number(fx, fy, zz), got1[a, slot])
            to_second(a, fx, fy, zz).start()

    @pl.loop(0, lines)
    def _(zz):
        for a in range(2):
            to_first(a, 0, 0, zz).wait_recv()
            slot = (x if a == 0 else y) * lines + zz
            add(a, number(0, 0, zz), got1[a, slot])

    def both(do):
        for up, down in zip(range(lines - 1, 0, -1), range(lines - 1)):

            @pl.when(z < up)
            def _():
                for a in range(2):
                    do(a, up, True)

            @pl.when(z > down)
            def _():
                for a in range(2):
                    do(a, down, False)

    def pass_on(a, zz, rising):
        to_second(a, 0, 0, zz).wait_recv()
        q = number(0, 0, zz)
        add(a, q, got2[a, zz])
        if rising:

            @pl.when(z > 0)
            def _():
                to_up(a, zz).wait_recv()
                add(a, q, got_up[a, zz])

            to_up(a, zz).start()
        else:

            @pl.when(z < lines - 1)
            def _():
                to_down(a, zz).wait_recv()
                add(a, q, got_down[a, zz])

            to_down(a, zz).start()

    both(pass_on)
    gmix_ref[...] = tab_out[len(partners), here.expert]

    for a, (base, result) in enumerate(((tok_ref, mixed_ref), (up_ref, gtok_ref))):
        to_second(a, 0, 0, z).wait_recv()
        q = number(0, 0, z)
        add(a, q, got2[a, z])

        @pl.when(z > 0)
        def _():
            to_up(a, z).wait_recv()
            add(a, q, got_up[a, z])

        @pl.when(z < lines - 1)
        def _():
            to_down(a, z).wait_recv()
            add(a, q, got_down[a, z])

        result[...] = (base[...].astype(jnp.float32) + acc[a, q].astype(jnp.float32)).astype(
            jnp.bfloat16
        )

    @pl.loop(0, lines)
    def _(zz):
        for a in range(2):
            for fx in (0, 1):
                for fy in (0, 1):
                    to_mate(a, fx, fy, zz).wait_send()
                    if fy if a == 0 else fx:
                        to_first(a, fx, fy, zz).wait_send()
            to_second(a, 1 - a, a, zz).wait_send()

    both(lambda a, zz, rising: (to_up(a, zz) if rising else to_down(a, zz)).wait_send())
    for i in range(len(partners)):
        table_copy(i).wait_send()


def return_rows(part_y, part_z, select, inner, tokens, upstream, sections, experts, cap):
    rows, width = tokens.shape
    lines, half = sections // 2, sections * experts // 2
    turned = select.reshape(experts, cap, rows).transpose(0, 2, 1)
    steps = 3 + (lines - 1).bit_length()
    vmem = pl.BlockSpec(memory_space=pltpu.VMEM)
    dma = pltpu.SemaphoreType.DMA

    def blocks(count):
        return pltpu.VMEM((2, count, rows, width), jnp.bfloat16)

    return pl.pallas_call(
        functools.partial(return_kernel, sections, experts, cap),
        out_shape=(
            jax.ShapeDtypeStruct(tokens.shape, jnp.bfloat16),
            jax.ShapeDtypeStruct(tokens.shape, jnp.bfloat16),
            jax.ShapeDtypeStruct((8, rows), jnp.float32),
        ),
        in_specs=[vmem] * 7,
        out_specs=[vmem] * 3,
        scratch_shapes=[
            blocks(half), blocks(half), blocks(half), blocks(sections), blocks(lines),
            blocks(lines), blocks(lines),
            pltpu.VMEM((steps + 1, experts, 8, rows), jnp.float32),
            pltpu.VMEM((steps, experts, 8, rows), jnp.float32),
            dma((2, half)), dma((2, half)), dma((2, sections)), dma((2, sections)),
            dma((2, lines)), dma((2, lines)), dma((2, lines)), dma((2, lines)),
            dma((2, lines)), dma((2, lines)), dma((steps,)), dma((steps,)),
        ],
        compiler_params=pltpu.CompilerParams(
            collective_id=1, has_side_effects=True, vmem_limit_bytes=VMEM_BYTES
        ),
        name="return_rows",
    )(part_y, part_z, select, turned, inner, tokens, upstream)


def slot_targets(route_rows, capacity, experts):
    tok_count, top_count = route_rows.shape
    flat_routes = route_rows.reshape(-1)
    onehot = (flat_routes[:, None] == jnp.arange(experts, dtype=jnp.int32)[None, :]).astype(
        jnp.int32
    )
    earlier = jnp.cumsum(onehot, axis=0) - onehot
    position = jnp.sum(earlier * onehot, axis=1)
    return (flat_routes * capacity + position).reshape(tok_count, top_count)


def across(a, b):
    return lax.dot_general(a, b, (((1,), (1,)), ((), ())), preferred_element_type=jnp.float32)


def down(a, b):
    return lax.dot_general(
        a, b, (((0,), (0,)), ((), ())), preferred_element_type=jnp.float32
    ).astype(jnp.bfloat16)


def by_tokens(tokens, routes, mix_weights, w_gate, w_up, w_down, upstream):
    experts, sections = lax.axis_size("expert"), lax.axis_size("section")
    tok_count, top_count = routes.shape
    capacity = 5 * tok_count * top_count // (4 * experts)
    target = slot_targets(routes, capacity, experts)
    meta = jnp.concatenate(
        [target.T.astype(jnp.float32), mix_weights.T, jnp.zeros((4, tok_count), jnp.float32)]
    )
    rows_in, rows_up, select, scale = gather_rows(
        meta, tokens, upstream, sections, experts, capacity
    )
    gate_local, up_local, down_local = w_gate[0], w_up[0], w_down[0]
    act_gate = jnp.dot(rows_in, gate_local, preferred_element_type=jnp.float32)
    act_up = jnp.dot(rows_in, up_local, preferred_element_type=jnp.float32)
    raw = across(rows_up, down_local)
    sig = jax.nn.sigmoid(act_gate)
    silu_gate = act_gate * sig
    hidden = silu_gate * act_up
    inner = jnp.sum(hidden * raw, axis=1, keepdims=True)
    hidden = (hidden * scale).astype(jnp.bfloat16)
    grad_hidden = raw * scale
    dsilu = sig * (1.0 + act_gate * (1.0 - sig))
    grad_act_gate = (grad_hidden * act_up * dsilu).astype(jnp.bfloat16)
    grad_act_up = (grad_hidden * silu_gate).astype(jnp.bfloat16)
    part_y = jnp.dot(hidden, down_local, preferred_element_type=jnp.float32).astype(jnp.bfloat16)
    part_z = (across(grad_act_gate, gate_local) + across(grad_act_up, up_local)).astype(
        jnp.bfloat16
    )
    grad_down = down(hidden, rows_up)
    grad_gate = down(rows_in, grad_act_gate)
    grad_up = down(rows_in, grad_act_up)
    mixed, grad_tokens, table = return_rows(
        part_y, part_z, select, inner, tokens, upstream, sections, experts, capacity
    )
    chosen = routes[:, :, None] == jnp.arange(experts, dtype=jnp.int32)
    grad_mix = jnp.sum(jnp.where(chosen, table[:experts].T[:, None, :], 0.0), axis=2)
    return (mixed, grad_tokens, grad_mix, grad_gate[None], grad_up[None], grad_down[None])


def slot_tables(route_rows, mix_rows, capacity, experts):
    tok_count, top_count = route_rows.shape
    flat_routes = route_rows.reshape(-1)
    onehot = (flat_routes[:, None] == jnp.arange(experts, dtype=jnp.int32)[None, :]).astype(
        jnp.int32
    )
    earlier = jnp.cumsum(onehot, axis=0) - onehot
    position = jnp.sum(earlier * onehot, axis=1)
    target = (flat_routes * capacity + position).reshape(tok_count, top_count)
    slot_ids = jnp.arange(experts * capacity, dtype=jnp.int32)
    hits = target[None, :, :] == slot_ids[:, None, None]
    matches = hits.astype(jnp.float32)
    select = jnp.sum(matches, axis=2)
    weighted = jnp.sum(matches * mix_rows[None, :, :], axis=2)
    token_ids = jnp.arange(tok_count, dtype=jnp.int32)
    slot_token = jnp.sum(jnp.sum(hits.astype(jnp.int32), axis=2) * token_ids[None, :], axis=1)
    return (target, select, weighted, slot_token)


def by_slots(tokens, routes, mix_weights, w_gate, w_up, w_down, upstream):
    experts = lax.axis_size("expert")
    tok_count = tokens.shape[0]
    top_count = routes.shape[1]
    capacity = 5 * tok_count * top_count // (4 * experts)
    slot_total = experts * capacity
    target, select, weighted, slot_token = slot_tables(routes, mix_weights, capacity, experts)
    slot_fill = jnp.sum(select, axis=1)
    slot_scale = jnp.sum(weighted, axis=1)
    gate_local = w_gate[0]
    up_local = w_up[0]
    down_local = w_down[0]

    def collect(source, factor):
        taken = source[slot_token].astype(jnp.float32)
        return (taken * factor[:, None]).astype(jnp.bfloat16)

    def to_experts(source, factor):
        block = collect(source, factor)
        arrived = lax.all_to_all(
            block.reshape(experts, capacity, -1), "expert", split_axis=0, concat_axis=0, tiled=True
        )
        whole = lax.all_gather(arrived, "section", axis=2, tiled=True)
        return whole.reshape(slot_total, -1)

    def to_sources(partial_value):
        summed = lax.psum_scatter(
            partial_value.reshape(experts, capacity, -1).astype(jnp.bfloat16),
            "section",
            scatter_dimension=2,
            tiled=True,
        )
        back = lax.all_to_all(summed, "expert", split_axis=0, concat_axis=0, tiled=True)
        return back.reshape(slot_total, -1)

    dispatched = to_experts(tokens, slot_fill)
    act_gate = jnp.dot(dispatched, gate_local, preferred_element_type=jnp.float32)
    act_up = jnp.dot(dispatched, up_local, preferred_element_type=jnp.float32)
    sig = jax.nn.sigmoid(act_gate)
    silu_gate = act_gate * sig
    hidden = (silu_gate * act_up).astype(jnp.bfloat16)
    partial_value = jnp.dot(hidden, down_local, preferred_element_type=jnp.float32)
    returned = to_sources(partial_value).astype(jnp.float32)
    moe_out = jnp.dot(weighted.T, returned, precision=highest)
    mixed = (tokens.astype(jnp.float32) + moe_out).astype(jnp.bfloat16)
    picked = returned[target]
    upstream_wide = upstream.astype(jnp.float32)
    mix_terms = jnp.einsum("tkd,td->tk", picked, upstream_wide, precision=highest)
    grad_mix = lax.psum(mix_terms, "section")
    grad_rows = to_experts(upstream, slot_scale)
    grad_hidden = lax.dot_general(
        grad_rows, down_local, (((1,), (1,)), ((), ())), preferred_element_type=jnp.float32
    )
    grad_down = lax.dot_general(
        hidden, grad_rows, (((0,), (0,)), ((), ())), preferred_element_type=jnp.float32
    ).astype(jnp.bfloat16)
    dsilu = sig * (1.0 + act_gate * (1.0 - sig))
    grad_act_gate = (grad_hidden * act_up * dsilu).astype(jnp.bfloat16)
    grad_act_up = (grad_hidden * silu_gate).astype(jnp.bfloat16)
    grad_gate = lax.dot_general(
        dispatched, grad_act_gate, (((0,), (0,)), ((), ())), preferred_element_type=jnp.float32
    ).astype(jnp.bfloat16)
    grad_up = lax.dot_general(
        dispatched, grad_act_up, (((0,), (0,)), ((), ())), preferred_element_type=jnp.float32
    ).astype(jnp.bfloat16)
    first = lax.dot_general(
        grad_act_gate, gate_local, (((1,), (1,)), ((), ())), preferred_element_type=jnp.float32
    )
    second = lax.dot_general(
        grad_act_up, up_local, (((1,), (1,)), ((), ())), preferred_element_type=jnp.float32
    )
    back_rows = to_sources(first + second).astype(jnp.float32)
    grad_moe = jnp.dot(select.T, back_rows, precision=highest)
    grad_tokens = (upstream_wide + grad_moe).astype(jnp.bfloat16)
    return (mixed, grad_tokens, grad_mix, grad_gate[None], grad_up[None], grad_down[None])


def per_device(*arrays):
    tokens, routes = arrays[:2]
    experts = lax.axis_size("expert")
    slots = 5 * tokens.shape[0] * routes.shape[1] // 4
    if experts * tokens.shape[0] <= 2 * slots:
        return by_tokens(*arrays)
    return by_slots(*arrays)


def solution(mesh):
    return jax.shard_map(
        per_device,
        mesh=mesh,
        in_specs=(
            P("expert", "section"),
            P("expert", None),
            P("expert", None),
            P("expert", None, "section"),
            P("expert", None, "section"),
            P("expert", "section", None),
            P("expert", "section"),
        ),
        out_specs=(
            P("expert", "section"),
            P("expert", "section"),
            P("expert", None),
            P("expert", None, "section"),
            P("expert", None, "section"),
            P("expert", "section", None),
        ),
        check_vma=False,
    )
```
